256 devices in a mesh: expert: 128 (over x, y, z_hi, core), hidden: 2 (over z_lo).
Axes of the slice: x: 4, y: 4, z: 8 (z_hi: 4, z_lo: 2; z = z_hi * 2 + z_lo), core: 2. Of those that a mesh axis runs over, the one named last changes fastest.
Arguments:
- tokens: bfloat16 [512, 196, 1024], P(('expert', 'hidden')), may hold values from -18 to 18
- grad_out: bfloat16 [512, 196, 1024], P(('expert', 'hidden')), may hold values from -192 to 192
- slot_weight: bfloat16 [1024, 128], replicated, may hold values from -3 to 3
- in_weight: bfloat16 [128, 1024, 4096], P('expert', None, 'hidden'), may hold values from -0.1875 to 0.1875
- out_weight: bfloat16 [128, 4096, 1024], P('expert', 'hidden'), may hold values from -0.09375 to 0.09375
Outputs:
- input_grad: bfloat16 [512, 196, 1024], P(('expert', 'hidden'))
- phi_grad: float32 [1024, 128], P(('expert', 'hidden'))
The draws below stay inside these ranges and needn't reach their ends.
All inputs are finite; a program needn't handle non-finite values.
Results may differ from the reference program's by a relative error of at most 0.025.
Values may be sent and summed in bfloat16 or wider, within the bound.
No kernel may reach another device: no remote copies, remote signals or barrier semaphores. Data moves between devices by JAX's collectives and lax.ppermute only.
A program may use at most 128 MiB of HBM per device.

```python
import jax
import jax.numpy as jnp
from jax import lax

D = 1024
FF = 4096
TOKENS_IMG = 196
IMG_DEV = 2
EXPERTS = 128
GROUPS = 256
IMAGES = 512


def draw_tokens(key, part):
    key = jax.random.fold_in(key, 3)
    subkeys = jax.random.split(key, 3)
    tok_shape = (IMAGES, TOKENS_IMG, D)
    values = jnp.clip(jax.random.normal(subkeys[0], tok_shape), -6.0, 6.0)
    owners = jax.random.permutation(subkeys[2], GROUPS)
    image_block = jnp.arange(IMAGES) // IMG_DEV
    feature_block = jnp.arange(D) // (D // GROUPS)
    boost = jnp.where(owners[image_block][:, None] == feature_block[None, :], 3.0, 1.0)
    values = values * boost[:, None, :]
    return values.astype(jnp.bfloat16)


def draw_slot_weight(key, part):
    key = jax.random.fold_in(key, 5)
    values = jnp.clip(jax.random.normal(key, (D, EXPERTS)), -6.0, 6.0) * 0.08
    return values.astype(jnp.bfloat16)


def block_levels(own_key, extent, pieces, least, high):
    def one(axis_at, parts):
        draws = jax.random.uniform(jax.random.fold_in(jax.random.fold_in(own_key, 6), axis_at), (parts,), jnp.float32, least / len(pieces), high / len(pieces))
        return jnp.repeat(jnp.exp(draws), extent[axis_at] // parts).reshape((-1,) + (1,) * (len(extent) - axis_at - 1))

    factor_of = one(*pieces[0])
    for cut in pieces[1:]:
        factor_of = factor_of * one(*cut)
    return factor_of


def scatter_about(key, extent, width, reach, pieces=(), dtype=jnp.bfloat16):
    gain = block_levels(key, extent, pieces, -0.22, 0.18) if pieces else 1.0
    values = jax.random.normal(key, extent, jnp.float32) * width * gain
    return jnp.minimum(jnp.maximum(values, -reach), reach).astype(dtype)


def setup_inputs(seed: int = 0) -> dict:
    seeds = jax.random.split(jax.random.key(seed), 6)
    tokens = draw_tokens(jax.random.fold_in(seeds[5], 71), 0)
    grad_out = scatter_about(seeds[1], (IMAGES, TOKENS_IMG, D), 32.0, 192.0, ((0, 256),))
    slot_weight = draw_slot_weight(jax.random.fold_in(seeds[5], 71), 0)
    in_weight = scatter_about(seeds[3], (EXPERTS, D, FF), D ** -0.5, 0.1875, ((0, 128), (2, 2)))
    out_weight = scatter_about(seeds[4], (EXPERTS, FF, D), FF ** -0.5, 0.09375, ((0, 128), (1, 2)))
    return {"tokens": tokens, "grad_out": grad_out, "slot_weight": slot_weight, "in_weight": in_weight, "out_weight": out_weight}


def gelu_tanh(inputs):
    return jax.nn.gelu(inputs, approximate=True)

def expert_step(packed):
    slot_row, grad_row, first, second = packed
    pre_act = jnp.dot(slot_row, first, preferred_element_type=jnp.float32)
    activation = gelu_tanh(pre_act).astype(jnp.bfloat16)
    slot_out = jnp.dot(activation, second, preferred_element_type=jnp.float32).astype(jnp.bfloat16)
    act_grad = jnp.dot(grad_row, second.T, preferred_element_type=jnp.float32)
    primal, pullback = jax.vjp(gelu_tanh, pre_act)
    pre_grad = pullback(act_grad)[0].astype(jnp.bfloat16)
    slot_back = jnp.dot(pre_grad, first.T, preferred_element_type=jnp.float32).astype(jnp.bfloat16)
    return (slot_out, slot_back)

def reference(tokens, grad_out, slot_weight, in_weight, out_weight):
    tok_wide = tokens.astype(jnp.float32)
    out_wide = grad_out.astype(jnp.float32)
    phi_wide = slot_weight.astype(jnp.float32)
    logits = jnp.einsum('imd,dn->imn', tok_wide, phi_wide)
    dispatch = jax.nn.softmax(logits, axis=1)
    combine = jax.nn.softmax(logits, axis=2)
    dispatch_b = dispatch.astype(jnp.bfloat16)
    combine_b = combine.astype(jnp.bfloat16)
    slot_inputs = jnp.einsum('imn,imd->ind', dispatch_b.astype(jnp.float32), tok_wide).astype(jnp.bfloat16)
    slot_grads = jnp.einsum('imn,imd->ind', combine_b.astype(jnp.float32), out_wide).astype(jnp.bfloat16)
    slot_out, slot_back = lax.map(expert_step, (jnp.transpose(slot_inputs, (1, 0, 2)), jnp.transpose(slot_grads, (1, 0, 2)), in_weight, out_weight))
    slot_outputs = jnp.transpose(slot_out, (1, 0, 2)).astype(jnp.float32)
    slot_in_grad = jnp.transpose(slot_back, (1, 0, 2)).astype(jnp.float32)
    combine_dw = jnp.einsum('imd,ind->imn', out_wide, slot_outputs)
    combine_dl = combine * (combine_dw - lax.optimization_barrier(jnp.sum(combine * combine_dw, axis=2, keepdims=True)))
    dispatch_dw = jnp.einsum('imd,ind->imn', tok_wide, slot_in_grad)
    dispatch_dl = dispatch * (dispatch_dw - lax.optimization_barrier(jnp.sum(dispatch * dispatch_dw, axis=1, keepdims=True)))
    logit_grad = (combine_dl + dispatch_dl).astype(jnp.bfloat16)
    logit_wide = logit_grad.astype(jnp.float32)
    input_grad = jnp.einsum('imn,ind->imd', dispatch_b.astype(jnp.float32), slot_in_grad) + jnp.einsum('imn,dn->imd', logit_wide, phi_wide)
    phi_grad = jnp.einsum('imd,imn->dn', tok_wide, logit_wide)
    return (input_grad.astype(jnp.bfloat16), phi_grad)
```

```python
import jax
import jax.numpy as jnp
from jax import lax
from jax.sharding import PartitionSpec as P


BOTH = ("expert", "hidden")


def gelu_tanh(inputs):
    return jax.nn.gelu(inputs, approximate=True)


def expert_pass(row_inputs, row_grads, first, second):
    pre_act = jnp.einsum("rkd,kdf->rkf", row_inputs, first, preferred_element_type=jnp.float32)
    activation = gelu_tanh(pre_act).astype(jnp.bfloat16)
    partial_out = jnp.einsum("rkf,kfd->rkd", activation, second, preferred_element_type=jnp.float32)
    act_grad = jnp.einsum("rkd,kfd->rkf", row_grads, second, preferred_element_type=jnp.float32)
    primal, pullback = jax.vjp(gelu_tanh, pre_act)
    pre_grad = pullback(act_grad)[0].astype(jnp.bfloat16)
    partial_back = jnp.einsum("rkf,kdf->rkd", pre_grad, first, preferred_element_type=jnp.float32)
    return (partial_out, partial_back)


def local(tokens, grad_out, slot_weight, in_weight, out_weight):
    logits = jnp.einsum("imd,dn->imn", tokens, slot_weight, preferred_element_type=jnp.float32)
    dispatch = jax.nn.softmax(logits, axis=1)
    combine = jax.nn.softmax(logits, axis=2)
    dispatch_b = dispatch.astype(jnp.bfloat16)
    combine_b = combine.astype(jnp.bfloat16)
    slot_inputs = jnp.einsum(
        "imn,imd->ind", dispatch_b, tokens, preferred_element_type=jnp.float32
    ).astype(jnp.bfloat16)
    slot_grads = jnp.einsum(
        "imn,imd->ind", combine_b, grad_out, preferred_element_type=jnp.float32
    ).astype(jnp.bfloat16)
    both = jnp.stack([slot_inputs, slot_grads], axis=0)
    both = jnp.transpose(both, (2, 0, 1, 3))
    experts, _, images, width = both.shape
    pairs = jnp.broadcast_to(both[:, None], (experts, 2, 2, images, width))
    pairs = pairs.reshape(2 * experts, 2, images, width)
    rows = lax.all_to_all(pairs, BOTH, split_axis=0, concat_axis=0, tiled=True)
    row_inputs = rows[:, 0].reshape(-1, 1, width)
    row_grads = rows[:, 1].reshape(-1, 1, width)
    partial_out, partial_back = expert_pass(row_inputs, row_grads, in_weight, out_weight)
    parts = jnp.stack(
        [
            partial_out.astype(jnp.bfloat16).reshape(-1, images, width),
            partial_back.astype(jnp.bfloat16).reshape(-1, images, width),
        ],
        axis=1,
    )
    halves = lax.all_to_all(parts, BOTH, split_axis=0, concat_axis=0, tiled=True)
    halves = halves.reshape(experts, 2, 2, images, width).astype(jnp.float32)
    summed = (halves[:, 0] + halves[:, 1]).astype(jnp.bfloat16)
    slot_outputs = jnp.transpose(summed[:, 0], (1, 0, 2))
    slot_in_grad = jnp.transpose(summed[:, 1], (1, 0, 2))
    combine_dw = jnp.einsum(
        "imd,ind->imn", grad_out, slot_outputs, preferred_element_type=jnp.float32
    )
    combine_dl = combine * (combine_dw - jnp.sum(combine * combine_dw, axis=2, keepdims=True))
    dispatch_dw = jnp.einsum(
        "imd,ind->imn", tokens, slot_in_grad, preferred_element_type=jnp.float32
    )
    dispatch_dl = dispatch * (dispatch_dw - jnp.sum(dispatch * dispatch_dw, axis=1, keepdims=True))
    logit_grad = (combine_dl + dispatch_dl).astype(jnp.bfloat16)
    input_grad = jnp.einsum(
        "imn,ind->imd", dispatch_b, slot_in_grad, preferred_element_type=jnp.float32
    )
    input_grad = input_grad + jnp.einsum(
        "imn,dn->imd", logit_grad, slot_weight, preferred_element_type=jnp.float32
    )
    phi_term = jnp.einsum("imd,imn->dn", tokens, logit_grad, preferred_element_type=jnp.float32)
    phi_parts = phi_term.astype(jnp.bfloat16).reshape(2 * experts, -1, experts)
    phi_parts = lax.all_to_all(phi_parts, BOTH, split_axis=0, concat_axis=0, tiled=True)
    phi_grad = jnp.sum(phi_parts.astype(jnp.float32), axis=0)
    return (input_grad.astype(jnp.bfloat16), phi_grad)


def solution(mesh):
    placed = (
        P(("expert", "hidden"), None, None),
        P(("expert", "hidden"), None, None),
        P(),
        P("expert", None, "hidden"),
        P("expert", "hidden", None),
    )
    return jax.shard_map(
        local,
        mesh=mesh,
        in_specs=placed,
        out_specs=(P(("expert", "hidden"), None, None), P(("expert", "hidden"), None)),
        check_vma=False,
    )
```

```python
import jax
import jax.numpy as jnp
from jax import lax
from jax.experimental import pallas as pl
from jax.experimental.pallas import tpu as pltpu
from jax.sharding import Mesh
from jax.sharding import PartitionSpec as P

ALL = ("x", "y", "z", "core", "half")
PLANE = ("x", "y", "core")
RING = ("z", "half")
FAR, NEAR, WIDE = (2, -2), (-1, 1), (-3, 3)
GELU_A = 0.7978845608028654
GELU_B = 0.7978845608028654 * 0.044715


def hops(steps, back=False):
    pairs = [(i, (i + steps[i % 2]) % 8) for i in range(8)]
    return [(b, a) for a, b in pairs] if back else pairs


def swap(block):
    return lax.ppermute(block, "half", [(0, 1), (1, 0)])


def expert_kernel(count, *refs):
    blocks = refs[:count]
    first, second = refs[count], refs[count + 1]
    outs = refs[count + 2 : 2 * count + 2]
    rows, acc = refs[2 * count + 2 :]
    size = blocks[0].shape[1]
    step = pl.program_id(0)

    @pl.when(step == 0)
    def _():
        for at, block in enumerate(blocks):
            rows[:, at * size : (at + 1) * size, :] = block[...]
        acc[...] = jnp.zeros_like(acc)

    contract_last = (((1,), (1,)), ((), ()))
    pre = jnp.dot(rows[0], first[...], preferred_element_type=jnp.float32)
    act_grad = lax.dot_general(
        rows[1], second[...], contract_last, preferred_element_type=jnp.float32
    )
    square = pre * pre
    bent = jnp.tanh(pre * (GELU_A + GELU_B * square))
    gate = 0.5 + 0.5 * bent
    activation = (pre * gate).astype(jnp.bfloat16)
    slope = gate + (0.5 * pre) * (1.0 - bent * bent) * (GELU_A + 3.0 * GELU_B * square)
    pre_grad = (act_grad * slope).astype(jnp.bfloat16)
    acc[0] += jnp.dot(activation, second[...], preferred_element_type=jnp.float32)
    acc[1] += lax.dot_general(
        pre_grad, first[...], contract_last, preferred_element_type=jnp.float32
    )

    @pl.when(step == pl.num_programs(0) - 1)
    def _():
        for at, out in enumerate(outs):
            out[...] = acc[:, at * size : (at + 1) * size, :].astype(out.dtype)


def expert_pass(mine, other, first, second):
    blocks = mine + other
    count = len(blocks)
    _, size, width = blocks[0].shape
    hidden = first.shape[1]
    part = 512
    whole = pl.BlockSpec((2, size, width), lambda j: (0, 0, 0))
    out = pl.pallas_call(
        lambda *refs: expert_kernel(count, *refs),
        grid=(hidden // part,),
        in_specs=[whole] * count
        + [
            pl.BlockSpec((width, part), lambda j: (0, j)),
            pl.BlockSpec((part, width), lambda j: (j, 0)),
        ],
        out_specs=[whole] * count,
        out_shape=[jax.ShapeDtypeStruct((2, size, width), jnp.float32)] * len(mine)
        + [jax.ShapeDtypeStruct((2, size, width), jnp.bfloat16)] * len(other),
        scratch_shapes=[
            pltpu.VMEM((2, count * size, width), jnp.bfloat16),
            pltpu.VMEM((2, count * size, width), jnp.float32),
        ],
        compiler_params=pltpu.CompilerParams(vmem_limit_bytes=40 * 2**20),
        cost_estimate=pl.CostEstimate(
            flops=8 * count * size * width * hidden,
            bytes_accessed=4 * width * hidden,
            transcendentals=count * size * hidden,
        ),
        name="expert_rows",
    )(*blocks, first, second)
    return out[: len(mine)], out[len(mine) :]


def slot_order(slots):
    at = lax.broadcasted_iota(jnp.int32, (slots, slots), 1)
    turn = 1 - 2 * lax.axis_index("half")
    kind = at % 4
    shift = jnp.where(kind == 1, turn, jnp.where(kind == 2, -turn, jnp.where(kind == 3, 2, 0)))
    plane = at // 4
    owner = (plane // 2) * 8 + ((lax.axis_index("z") + shift + 4) % 4) * 2 + plane % 2
    return (lax.broadcasted_iota(jnp.int32, (slots, slots), 0) == owner).astype(jnp.bfloat16)


def local(tokens, grad_out, slot_weight, in_weight, out_weight):
    images, _, width = tokens.shape
    slots = slot_weight.shape[1]
    order = slot_order(slots)
    slot_weight = jnp.dot(
        slot_weight, order, preferred_element_type=jnp.float32
    ).astype(jnp.bfloat16)
    logits = jnp.einsum("imd,dn->imn", tokens, slot_weight, preferred_element_type=jnp.float32)
    dispatch = jax.nn.softmax(logits, axis=1)
    combine = jax.nn.softmax(logits, axis=2)
    dispatch_b = dispatch.astype(jnp.bfloat16)
    combine_b = combine.astype(jnp.bfloat16)
    slot_inputs = jnp.einsum(
        "imn,imd->ind", dispatch_b, tokens, preferred_element_type=jnp.float32
    ).astype(jnp.bfloat16)
    slot_grads = jnp.einsum(
        "imn,imd->ind", combine_b, grad_out, preferred_element_type=jnp.float32
    ).astype(jnp.bfloat16)
    both = jnp.transpose(jnp.stack([slot_inputs, slot_grads], axis=0), (2, 0, 1, 3))
    both = both.reshape(slots // 4, 4, 2, images, width)
    both = lax.all_to_all(both, PLANE, split_axis=0, concat_axis=0, tiled=True)
    both = jnp.transpose(both, (1, 2, 0, 3, 4)).reshape(4, 2, -1, width)

    far = lax.ppermute(both[1], RING, hops(FAR))
    wide = lax.ppermute(both[3], RING, hops(WIDE))
    near = lax.ppermute(both[2], RING, hops(NEAR))
    own = both[0]
    far_pair, wide_pair = swap(far), swap(wide)
    own_pair, near_pair = swap(own), swap(near)
    first, second = in_weight[0], out_weight[0]
    mine_a, other_a = expert_pass([wide, far], [wide_pair, far_pair], first, second)
    mine_b, other_b = expert_pass([own, near], [own_pair, near_pair], first, second)

    def added(partial, sent):
        return (partial + swap(sent).astype(jnp.float32)).astype(jnp.bfloat16)

    wide_sum, far_sum = (added(a, b) for a, b in zip(mine_a, other_a))
    own_sum, near_sum = (added(a, b) for a, b in zip(mine_b, other_b))
    wide_sum = lax.ppermute(wide_sum, RING, hops(WIDE, True))
    far_sum = lax.ppermute(far_sum, RING, hops(FAR, True))
    near_sum = lax.ppermute(near_sum, RING, hops(NEAR, True))
    sums = jnp.stack([own_sum, far_sum, near_sum, wide_sum], axis=0)
    sums = jnp.transpose(sums.reshape(4, 2, slots // 4, images, width), (2, 0, 1, 3, 4))
    sums = lax.all_to_all(sums, PLANE, split_axis=0, concat_axis=0, tiled=True)
    sums = jnp.transpose(sums.reshape(slots, 2, images, width), (1, 2, 0, 3))
    slot_outputs, slot_in_grad = sums[0], sums[1]

    combine_dw = jnp.einsum(
        "imd,ind->imn", grad_out, slot_outputs, preferred_element_type=jnp.float32
    )
    combine_dl = combine * (combine_dw - jnp.sum(combine * combine_dw, axis=2, keepdims=True))
    dispatch_dw = jnp.einsum(
        "imd,ind->imn", tokens, slot_in_grad, preferred_element_type=jnp.float32
    )
    dispatch_dl = dispatch * (dispatch_dw - jnp.sum(dispatch * dispatch_dw, axis=1, keepdims=True))
    logit_grad = (combine_dl + dispatch_dl).astype(jnp.bfloat16)
    input_grad = jnp.einsum(
        "imn,ind->imd", dispatch_b, slot_in_grad, preferred_element_type=jnp.float32
    )
    input_grad = input_grad + jnp.einsum(
        "imn,dn->imd", logit_grad, slot_weight, preferred_element_type=jnp.float32
    )
    phi_term = jnp.einsum("imd,imn->dn", tokens, logit_grad, preferred_element_type=jnp.float32)
    phi_term = lax.dot_general(
        phi_term.astype(jnp.bfloat16),
        order,
        (((1,), (1,)), ((), ())),
        preferred_element_type=jnp.float32,
    )
    parts = phi_term.astype(jnp.bfloat16).reshape(2 * slots, -1, slots)
    parts = lax.all_to_all(parts, ALL, split_axis=0, concat_axis=0, tiled=True)
    phi_grad = jnp.sum(parts.astype(jnp.float32), axis=0)
    return (input_grad.astype(jnp.bfloat16), phi_grad)


def solution(mesh):
    expert = ("x", "y", "z", "core")
    fine = Mesh(mesh.devices.reshape(4, 4, 4, 2, 2), ALL)
    placed = (
        P(ALL, None, None),
        P(ALL, None, None),
        P(),
        P(expert, None, "half"),
        P(expert, "half", None),
    )
    return jax.shard_map(
        local,
        mesh=fine,
        in_specs=placed,
        out_specs=(P(ALL, None, None), P(ALL, None)),
        check_vma=False,
    )
```

```python
import jax
import jax.numpy as jnp
from jax import lax
from jax.experimental import pallas as pl
from jax.experimental.pallas import tpu as pltpu
from jax.sharding import Mesh
from jax.sharding import PartitionSpec as P

ALL = ("x", "y", "z", "core", "half")
PLANE = ("x", "y", "core")
RING = ("z", "half")
FAR, NEAR, WIDE = (2, -2), (-1, 1), (-3, 3)
GELU_A = 0.7978845608028654
GELU_B = 0.7978845608028654 * 0.044715


def hops(steps, back=False):
    pairs = [(i, (i + steps[i % 2]) % 8) for i in range(8)]
    return [(b, a) for a, b in pairs] if back else pairs


def swap(block):
    return lax.ppermute(block, "half", [(0, 1), (1, 0)])


def after(value, *earlier):
    return lax.optimization_barrier((value,) + earlier)[0]


def expert_kernel(count, *refs):
    blocks = refs[:count]
    first, second = refs[count], refs[count + 1]
    outs = refs[count + 2 : 2 * count + 2]
    rows, acc = refs[2 * count + 2 :]
    size = blocks[0].shape[1]
    step = pl.program_id(0)

    @pl.when(step == 0)
    def _():
        for at, block in enumerate(blocks):
            rows[:, at * size : (at + 1) * size, :] = block[...]
        acc[...] = jnp.zeros_like(acc)

    contract_last = (((1,), (1,)), ((), ()))
    pre = jnp.dot(rows[0], first[...], preferred_element_type=jnp.float32)
    act_grad = lax.dot_general(
        rows[1], second[...], contract_last, preferred_element_type=jnp.float32
    )
    square = pre * pre
    bent = jnp.tanh(pre * (GELU_A + GELU_B * square))
    gate = 0.5 + 0.5 * bent
    activation = (pre * gate).astype(jnp.bfloat16)
    slope = gate + (0.5 * pre) * (1.0 - bent * bent) * (GELU_A + 3.0 * GELU_B * square)
    pre_grad = (act_grad * slope).astype(jnp.bfloat16)
    acc[0] += jnp.dot(activation, second[...], preferred_element_type=jnp.float32)
    acc[1] += lax.dot_general(
        pre_grad, first[...], contract_last, preferred_element_type=jnp.float32
    )

    @pl.when(step == pl.num_programs(0) - 1)
    def _():
        for at, out in enumerate(outs):
            out[...] = acc[:, at * size : (at + 1) * size, :].astype(out.dtype)


def expert_pass(mine, other, first, second):
    blocks = mine + other
    count = len(blocks)
    _, size, width = blocks[0].shape
    hidden = first.shape[1]
    part = 512
    whole = pl.BlockSpec((2, size, width), lambda j: (0, 0, 0))
    out = pl.pallas_call(
        lambda *refs: expert_kernel(count, *refs),
        grid=(hidden // part,),
        in_specs=[whole] * count
        + [
            pl.BlockSpec((width, part), lambda j: (0, j)),
            pl.BlockSpec((part, width), lambda j: (j, 0)),
        ],
        out_specs=[whole] * count,
        out_shape=[jax.ShapeDtypeStruct((2, size, width), jnp.float32)] * len(mine)
        + [jax.ShapeDtypeStruct((2, size, width), jnp.bfloat16)] * len(other),
        scratch_shapes=[
            pltpu.VMEM((2, count * size, width), jnp.bfloat16),
            pltpu.VMEM((2, count * size, width), jnp.float32),
        ],
        compiler_params=pltpu.CompilerParams(vmem_limit_bytes=24 * 2**20),
        cost_estimate=pl.CostEstimate(
            flops=8 * count * size * width * hidden,
            bytes_accessed=4 * width * hidden,
            transcendentals=count * size * hidden,
        ),
        name="expert_rows",
    )(*blocks, first, second)
    return out[: len(mine)], out[len(mine) :]


def slot_order(slots):
    at = lax.broadcasted_iota(jnp.int32, (slots, slots), 1)
    turn = 1 - 2 * lax.axis_index("half")
    kind = at % 4
    shift = jnp.where(kind == 1, turn, jnp.where(kind == 2, -turn, jnp.where(kind == 3, 2, 0)))
    plane = at // 4
    owner = (plane // 2) * 8 + ((lax.axis_index("z") + shift + 4) % 4) * 2 + plane % 2
    return (lax.broadcasted_iota(jnp.int32, (slots, slots), 0) == owner).astype(jnp.bfloat16)


def local(tokens, grad_out, slot_weight, in_weight, out_weight):
    images, _, width = tokens.shape
    slots = slot_weight.shape[1]
    order = slot_order(slots)
    slot_weight = jnp.dot(
        slot_weight, order, preferred_element_type=jnp.float32
    ).astype(jnp.bfloat16)
    logits = jnp.einsum("imd,dn->imn", tokens, slot_weight, preferred_element_type=jnp.float32)
    dispatch = jax.nn.softmax(logits, axis=1)
    combine = jax.nn.softmax(logits, axis=2)
    dispatch_b = dispatch.astype(jnp.bfloat16)
    combine_b = combine.astype(jnp.bfloat16)
    slot_inputs = jnp.einsum(
        "imn,imd->ind", dispatch_b, tokens, preferred_element_type=jnp.float32
    ).astype(jnp.bfloat16)
    slot_grads = jnp.einsum(
        "imn,imd->ind", combine_b, grad_out, preferred_element_type=jnp.float32
    ).astype(jnp.bfloat16)
    both = jnp.transpose(jnp.stack([slot_inputs, slot_grads], axis=0), (2, 0, 1, 3))
    both = both.reshape(slots // 4, 4, 2, images, width)
    both = lax.all_to_all(both, PLANE, split_axis=0, concat_axis=0, tiled=True)
    both = jnp.transpose(both, (1, 2, 0, 3, 4)).reshape(4, 2, -1, width)

    far = lax.ppermute(both[1], RING, hops(FAR))
    wide = lax.ppermute(both[3], RING, hops(WIDE))
    own = both[0]
    own_pair = swap(own)
    first, second = (
        pltpu.with_memory_space_constraint(weight[0], pltpu.HBM)
        for weight in (in_weight, out_weight)
    )
    near = lax.ppermute(after(both[2], far, wide), RING, hops(NEAR))
    far_pair, wide_pair = swap(far), swap(wide)
    near_pair = swap(near)
    mine_a, other_a = expert_pass([wide, far], [wide_pair, far_pair], first, second)
    back_a = [swap(sent) for sent in other_a]
    mine_b, other_b = expert_pass(
        [after(own, *mine_a), near], [own_pair, near_pair], first, second
    )
    back_b = [swap(after(sent, *back_a)) for sent in other_b]

    def added(partial, sent):
        return (partial + sent.astype(jnp.float32)).astype(jnp.bfloat16)

    wide_sum, far_sum = (added(a, b) for a, b in zip(mine_a, back_a))
    own_sum, near_sum = (added(a, b) for a, b in zip(mine_b, back_b))
    wide_sum = lax.ppermute(wide_sum, RING, hops(WIDE, True))
    far_sum = lax.ppermute(far_sum, RING, hops(FAR, True))
    near_sum = lax.ppermute(near_sum, RING, hops(NEAR, True))
    sums = jnp.stack([own_sum, far_sum, near_sum, wide_sum], axis=0)
    sums = jnp.transpose(sums.reshape(4, 2, slots // 4, images, width), (2, 0, 1, 3, 4))
    sums = lax.all_to_all(sums, PLANE, split_axis=0, concat_axis=0, tiled=True)
    sums = jnp.transpose(sums.reshape(slots, 2, images, width), (1, 2, 0, 3))
    slot_outputs, slot_in_grad = sums[0], sums[1]

    combine_dw = jnp.einsum(
        "imd,ind->imn", grad_out, slot_outputs, preferred_element_type=jnp.float32
    )
    combine_dl = combine * (combine_dw - jnp.sum(combine * combine_dw, axis=2, keepdims=True))
    dispatch_dw = jnp.einsum(
        "imd,ind->imn", tokens, slot_in_grad, preferred_element_type=jnp.float32
    )
    dispatch_dl = dispatch * (dispatch_dw - jnp.sum(dispatch * dispatch_dw, axis=1, keepdims=True))
    logit_grad = (combine_dl + dispatch_dl).astype(jnp.bfloat16)
    input_grad = jnp.einsum(
        "imn,ind->imd", dispatch_b, slot_in_grad, preferred_element_type=jnp.float32
    )
    input_grad = input_grad + jnp.einsum(
        "imn,dn->imd", logit_grad, slot_weight, preferred_element_type=jnp.float32
    )
    phi_term = jnp.einsum("imd,imn->dn", tokens, logit_grad, preferred_element_type=jnp.float32)
    phi_term = lax.dot_general(
        phi_term.astype(jnp.bfloat16),
        order,
        (((1,), (1,)), ((), ())),
        preferred_element_type=jnp.float32,
    )
    parts = phi_term.astype(jnp.bfloat16).reshape(2 * slots, -1, slots)
    parts = lax.all_to_all(parts, ALL, split_axis=0, concat_axis=0, tiled=True)
    phi_grad = jnp.sum(parts.astype(jnp.float32), axis=0)
    return (input_grad.astype(jnp.bfloat16), phi_grad)


def solution(mesh):
    expert = ("x", "y", "z", "core")
    fine = Mesh(mesh.devices.reshape(4, 4, 4, 2, 2), ALL)
    placed = (
        P(ALL, None, None),
        P(ALL, None, None),
        P(),
        P(expert, None, "half"),
        P(expert, "half", None),
    )
    return jax.shard_map(
        local,
        mesh=fine,
        in_specs=placed,
        out_specs=(P(ALL, None, None), P(ALL, None)),
        check_vma=False,
    )
```

```python
import jax
import jax.numpy as jnp
from jax import lax
from jax.experimental import pallas as pl
from jax.experimental.pallas import tpu as pltpu
from jax.sharding import PartitionSpec as P

BOTH = ("expert", "hidden")
GELU_A = 0.7978845608028654
GELU_B = 0.7978845608028654 * 0.044715


def swap(block):
    return lax.ppermute(block, "hidden", [(0, 1), (1, 0)])


def after(value, *earlier):
    return lax.optimization_barrier((value,) + earlier)[0]


def expert_kernel(count, *refs):
    blocks = refs[:count]
    first, second = refs[count], refs[count + 1]
    outs = refs[count + 2 : 2 * count + 2]
    rows, acc = refs[2 * count + 2 :]
    size = blocks[0].shape[1]
    step = pl.program_id(0)

    @pl.when(step == 0)
    def _():
        for at, block in enumerate(blocks):
            rows[:, at * size : (at + 1) * size, :] = block[...]
        acc[...] = jnp.zeros_like(acc)

    contract_last = (((1,), (1,)), ((), ()))
    pre = jnp.dot(rows[0], first[...], preferred_element_type=jnp.float32)
    act_grad = lax.dot_general(
        rows[1], second[...], contract_last, preferred_element_type=jnp.float32
    )
    square = pre * pre
    bent = jnp.tanh(pre * (GELU_A + GELU_B * square))
    gate = 0.5 + 0.5 * bent
    activation = (pre * gate).astype(jnp.bfloat16)
    slope = gate + (0.5 * pre) * (1.0 - bent * bent) * (GELU_A + 3.0 * GELU_B * square)
    pre_grad = (act_grad * slope).astype(jnp.bfloat16)
    acc[0] += jnp.dot(activation, second[...], preferred_element_type=jnp.float32)
    acc[1] += lax.dot_general(
        pre_grad, first[...], contract_last, preferred_element_type=jnp.float32
    )

    @pl.when(step == pl.num_programs(0) - 1)
    def _():
        for at, out in enumerate(outs):
            out[...] = acc[:, at * size : (at + 1) * size, :].astype(out.dtype)


def expert_pass(blocks, dtype, first, second):
    count = len(blocks)
    _, size, width = blocks[0].shape
    hidden = first.shape[1]
    part = 512
    whole = pl.BlockSpec((2, size, width), lambda j: (0, 0, 0))
    return pl.pallas_call(
        lambda *refs: expert_kernel(count, *refs),
        grid=(hidden // part,),
        in_specs=[whole] * count
        + [
            pl.BlockSpec((width, part), lambda j: (0, j)),
            pl.BlockSpec((part, width), lambda j: (j, 0)),
        ],
        out_specs=[whole] * count,
        out_shape=[jax.ShapeDtypeStruct((2, size, width), dtype)] * count,
        scratch_shapes=[
            pltpu.VMEM((2, count * size, width), jnp.bfloat16),
            pltpu.VMEM((2, count * size, width), jnp.float32),
        ],
        compiler_params=pltpu.CompilerParams(vmem_limit_bytes=24 * 2**20),
        cost_estimate=pl.CostEstimate(
            flops=8 * count * size * width * hidden,
            bytes_accessed=4 * width * hidden,
            transcendentals=count * size * hidden,
        ),
        name="expert_rows",
    )(*blocks, first, second)


def local(tokens, grad_out, slot_weight, in_weight, out_weight):
    images = tokens.shape[0]
    logits = jnp.einsum("imd,dn->imn", tokens, slot_weight, preferred_element_type=jnp.float32)
    dispatch = jax.nn.softmax(logits, axis=1)
    combine = jax.nn.softmax(logits, axis=2)
    dispatch_b = dispatch.astype(jnp.bfloat16)
    combine_b = combine.astype(jnp.bfloat16)
    slot_inputs = jnp.einsum(
        "imn,imd->ind", dispatch_b, tokens, preferred_element_type=jnp.float32
    ).astype(jnp.bfloat16)
    slot_grads = jnp.einsum(
        "imn,imd->ind", combine_b, grad_out, preferred_element_type=jnp.float32
    ).astype(jnp.bfloat16)
    both = jnp.stack([slot_inputs, slot_grads], axis=0)
    both = jnp.transpose(both, (2, 0, 1, 3))
    experts, _, _, width = both.shape
    both = lax.all_to_all(both, "expert", split_axis=0, concat_axis=0, tiled=True)
    both = jnp.transpose(both.reshape(2, experts // 2, 2, images, width), (0, 2, 1, 3, 4))
    both = both.reshape(2, 2, -1, width)
    first, second = (
        pltpu.with_memory_space_constraint(weight[0], pltpu.HBM)
        for weight in (in_weight, out_weight)
    )
    pair_a = swap(both[0])
    mine = expert_pass([both[0], both[1]], jnp.float32, first, second)
    pair_b = swap(after(both[1], mine[0]))
    (sent_a,) = expert_pass([pair_a], jnp.bfloat16, first, second)
    back_a = swap(sent_a)
    (sent_b,) = expert_pass([pair_b], jnp.bfloat16, first, second)
    back_b = swap(sent_b)
    sums = [
        (partial + back.astype(jnp.float32)).astype(jnp.bfloat16)
        for partial, back in zip(mine, (back_a, back_b))
    ]
    sums = jnp.stack(sums, axis=0).reshape(2, 2, experts // 2, images, width)
    sums = jnp.transpose(sums, (0, 2, 1, 3, 4)).reshape(experts, 2, images, width)
    summed = lax.all_to_all(sums, "expert", split_axis=0, concat_axis=0, tiled=True)
    slot_outputs = jnp.transpose(summed[:, 0], (1, 0, 2))
    slot_in_grad = jnp.transpose(summed[:, 1], (1, 0, 2))
    combine_dw = jnp.einsum(
        "imd,ind->imn", grad_out, slot_outputs, preferred_element_type=jnp.float32
    )
    combine_dl = combine * (combine_dw - jnp.sum(combine * combine_dw, axis=2, keepdims=True))
    dispatch_dw = jnp.einsum(
        "imd,ind->imn", tokens, slot_in_grad, preferred_element_type=jnp.float32
    )
    dispatch_dl = dispatch * (dispatch_dw - jnp.sum(dispatch * dispatch_dw, axis=1, keepdims=True))
    logit_grad = (combine_dl + dispatch_dl).astype(jnp.bfloat16)
    input_grad = jnp.einsum(
        "imn,ind->imd", dispatch_b, slot_in_grad, preferred_element_type=jnp.float32
    )
    input_grad = input_grad + jnp.einsum(
        "imn,dn->imd", logit_grad, slot_weight, preferred_element_type=jnp.float32
    )
    phi_term = jnp.einsum("imd,imn->dn", tokens, logit_grad, preferred_element_type=jnp.float32)
    phi_parts = phi_term.astype(jnp.bfloat16).reshape(2 * experts, -1, experts)
    phi_parts = lax.all_to_all(phi_parts, BOTH, split_axis=0, concat_axis=0, tiled=True)
    phi_grad = jnp.sum(phi_parts.astype(jnp.float32), axis=0)
    return (input_grad.astype(jnp.bfloat16), phi_grad)


def solution(mesh):
    placed = (
        P(("expert", "hidden"), None, None),
        P(("expert", "hidden"), None, None),
        P(),
        P("expert", None, "hidden"),
        P("expert", "hidden", None),
    )
    return jax.shard_map(
        local,
        mesh=mesh,
        in_specs=placed,
        out_specs=(P(("expert", "hidden"), None, None), P(("expert", "hidden"), None)),
        check_vma=False,
    )
```

```python
import jax
import jax.numpy as jnp
from jax import lax
from jax.experimental import pallas as pl
from jax.experimental.pallas import tpu as pltpu
from jax.sharding import PartitionSpec as P

BOTH = ("expert", "hidden")
GELU_A = 0.7978845608028654
GELU_B = 0.7978845608028654 * 0.044715


def swap(block):
    return lax.ppermute(block, "hidden", [(0, 1), (1, 0)])


def after(value, *earlier):
    return lax.optimization_barrier((value,) + earlier)[0]


def expert_kernel(count, *refs):
    blocks = refs[:count]
    first, second = refs[count], refs[count + 1]
    outs = refs[count + 2 : 2 * count + 2]
    rows, acc = refs[2 * count + 2 :]
    size = blocks[0].shape[1]
    step = pl.program_id(0)

    @pl.when(step == 0)
    def _():
        for at, block in enumerate(blocks):
            rows[:, at * size : (at + 1) * size, :] = block[...]
        acc[...] = jnp.zeros_like(acc)

    contract_last = (((1,), (1,)), ((), ()))
    pre = jnp.dot(rows[0], first[...], preferred_element_type=jnp.float32)
    act_grad = lax.dot_general(
        rows[1], second[...], contract_last, preferred_element_type=jnp.float32
    )
    square = pre * pre
    bent = jnp.tanh(pre * (GELU_A + GELU_B * square))
    gate = 0.5 + 0.5 * bent
    activation = (pre * gate).astype(jnp.bfloat16)
    slope = gate + (0.5 * pre) * (1.0 - bent * bent) * (GELU_A + 3.0 * GELU_B * square)
    pre_grad = (act_grad * slope).astype(jnp.bfloat16)
    acc[0] += jnp.dot(activation, second[...], preferred_element_type=jnp.float32)
    acc[1] += lax.dot_general(
        pre_grad, first[...], contract_last, preferred_element_type=jnp.float32
    )

    @pl.when(step == pl.num_programs(0) - 1)
    def _():
        for at, out in enumerate(outs):
            out[...] = acc[:, at * size : (at + 1) * size, :].astype(out.dtype)


def expert_pass(blocks, dtype, first, second):
    count = len(blocks)
    _, size, width = blocks[0].shape
    hidden = first.shape[1]
    part = 512
    whole = pl.BlockSpec((2, size, width), lambda j: (0, 0, 0))
    return pl.pallas_call(
        lambda *refs: expert_kernel(count, *refs),
        grid=(hidden // part,),
        in_specs=[whole] * count
        + [
            pl.BlockSpec((width, part), lambda j: (0, j)),
            pl.BlockSpec((part, width), lambda j: (j, 0)),
        ],
        out_specs=[whole] * count,
        out_shape=[jax.ShapeDtypeStruct((2, size, width), dtype)] * count,
        scratch_shapes=[
            pltpu.VMEM((2, count * size, width), jnp.bfloat16),
            pltpu.VMEM((2, count * size, width), jnp.float32),
        ],
        compiler_params=pltpu.CompilerParams(vmem_limit_bytes=24 * 2**20),
        cost_estimate=pl.CostEstimate(
            flops=8 * count * size * width * hidden,
            bytes_accessed=4 * width * hidden,
            transcendentals=count * size * hidden,
        ),
        name="expert_rows",
    )(*blocks, first, second)


def sum_kernel(mine_a, back_a, mine_b, back_b, out):
    out[0] = (mine_a[...] + back_a[...].astype(jnp.float32)).astype(jnp.bfloat16)
    out[1] = (mine_b[...] + back_b[...].astype(jnp.float32)).astype(jnp.bfloat16)


def sum_halves(*parts):
    return pl.pallas_call(
        sum_kernel,
        out_shape=jax.ShapeDtypeStruct((2,) + parts[0].shape, jnp.bfloat16),
        compiler_params=pltpu.CompilerParams(vmem_limit_bytes=16 * 2**20),
        cost_estimate=pl.CostEstimate(
            flops=2 * parts[0].size, bytes_accessed=16 * parts[0].size, transcendentals=0
        ),
        name="sum_halves",
    )(*parts)


def grad_kernel(tokens, turned, grads, combine, dispatch, outs, backs, logit_grad, phi):
    contract_last = (((1,), (1,)), ((), ()))
    total = None
    for image in range(tokens.shape[0]):
        comb, disp = combine[image], dispatch[image]
        wide = lax.dot_general(
            grads[image], outs[image], contract_last, preferred_element_type=jnp.float32
        )
        deep = lax.dot_general(
            tokens[image], backs[image], contract_last, preferred_element_type=jnp.float32
        )
        wide = comb * (wide - jnp.sum(comb * wide, axis=1, keepdims=True))
        deep = disp * (deep - jnp.sum(disp * deep, axis=0, keepdims=True))
        grad = (wide + deep).astype(jnp.bfloat16)
        logit_grad[image] = grad
        term = jnp.dot(turned[image], grad, preferred_element_type=jnp.float32)
        total = term if total is None else total + term
    phi[...] = total.astype(jnp.bfloat16)


def logit_grads(tokens, turned, grads, combine, dispatch, outs, backs):
    images, rows, width = tokens.shape
    slots = outs.shape[1]
    return pl.pallas_call(
        grad_kernel,
        out_shape=[
            jax.ShapeDtypeStruct((images, rows, slots), jnp.bfloat16),
            jax.ShapeDtypeStruct((width, slots), jnp.bfloat16),
        ],
        compiler_params=pltpu.CompilerParams(vmem_limit_bytes=24 * 2**20),
        cost_estimate=pl.CostEstimate(
            flops=6 * images * rows * width * slots,
            bytes_accessed=8 * images * rows * width,
            transcendentals=0,
        ),
        name="logit_grads",
    )(tokens, turned, grads, combine, dispatch, outs, backs)


def local(tokens, grad_out, slot_weight, in_weight, out_weight):
    images = tokens.shape[0]
    logits = jnp.einsum("imd,dn->imn", tokens, slot_weight, preferred_element_type=jnp.float32)
    logits = lax.optimization_barrier(logits)
    dispatch = jax.nn.softmax(logits, axis=1)
    combine = jax.nn.softmax(logits, axis=2)
    dispatch_b = dispatch.astype(jnp.bfloat16)
    combine_b = combine.astype(jnp.bfloat16)
    slot_inputs = jnp.einsum(
        "imn,imd->ind", dispatch_b, tokens, preferred_element_type=jnp.float32
    ).astype(jnp.bfloat16)
    slot_grads = jnp.einsum(
        "imn,imd->ind", combine_b, grad_out, preferred_element_type=jnp.float32
    ).astype(jnp.bfloat16)
    both = jnp.stack([slot_inputs, slot_grads], axis=0)
    both = jnp.transpose(both, (2, 0, 1, 3))
    experts, _, _, width = both.shape
    both = lax.all_to_all(both, "expert", split_axis=0, concat_axis=0, tiled=True)
    both = jnp.transpose(both.reshape(2, experts // 2, 2, images, width), (0, 2, 1, 3, 4))
    both = both.reshape(2, 2, -1, width)
    first, second = (
        pltpu.with_memory_space_constraint(weight[0], pltpu.HBM)
        for weight in (in_weight, out_weight)
    )
    pair_a = swap(both[0])
    mine = expert_pass([both[0], both[1]], jnp.float32, first, second)
    pair_b = swap(after(both[1], mine[0]))
    flat_tokens, flat_grads, _ = lax.optimization_barrier((tokens, grad_out, mine[0]))
    turned = jnp.transpose(flat_tokens, (0, 2, 1))
    (sent_a,) = expert_pass([pair_a], jnp.bfloat16, first, second)
    back_a = swap(sent_a)
    (sent_b,) = expert_pass([pair_b], jnp.bfloat16, first, second)
    back_b = swap(sent_b)
    sums = sum_halves(mine[0], back_a, mine[1], back_b)
    sums = sums.reshape(2, 2, experts // 2, images, width)
    sums = jnp.transpose(sums, (0, 2, 1, 3, 4)).reshape(experts, 2, images, width)
    summed = lax.all_to_all(sums, "expert", split_axis=0, concat_axis=0, tiled=True)
    slot_outputs = jnp.transpose(summed[:, 0], (1, 0, 2))
    slot_in_grad = jnp.transpose(summed[:, 1], (1, 0, 2))
    logit_grad, phi_parts = logit_grads(
        flat_tokens, turned, flat_grads, combine, dispatch, slot_outputs, slot_in_grad
    )
    input_grad = jnp.einsum(
        "imn,ind->imd", dispatch_b, slot_in_grad, preferred_element_type=jnp.float32
    )
    input_grad = input_grad + jnp.einsum(
        "imn,dn->imd", logit_grad, slot_weight, preferred_element_type=jnp.float32
    )
    phi_parts = phi_parts.reshape(2 * experts, -1, experts)
    phi_parts = lax.all_to_all(phi_parts, BOTH, split_axis=0, concat_axis=0, tiled=True)
    phi_grad = jnp.sum(phi_parts.astype(jnp.float32), axis=0)
    return (input_grad.astype(jnp.bfloat16), phi_grad)


def solution(mesh):
    placed = (
        P(("expert", "hidden"), None, None),
        P(("expert", "hidden"), None, None),
        P(),
        P("expert", None, "hidden"),
        P("expert", "hidden", None),
    )
    return jax.shard_map(
        local,
        mesh=mesh,
        in_specs=placed,
        out_specs=(P(("expert", "hidden"), None, None), P(("expert", "hidden"), None)),
        check_vma=False,
    )
```

```python
import jax
import jax.numpy as jnp
from jax import lax
from jax.experimental import pallas as pl
from jax.experimental.pallas import tpu as pltpu
from jax.sharding import PartitionSpec as P

BOTH = ("expert", "hidden")
GELU_A = 0.7978845608028654
GELU_B = 0.7978845608028654 * 0.044715


def swap(block):
    return lax.ppermute(block, "hidden", [(0, 1), (1, 0)])


def after(value, *earlier):
    return lax.optimization_barrier((value,) + earlier)[0]


def expert_kernel(count, *refs):
    blocks = refs[:count]
    first, second = refs[count], refs[count + 1]
    outs = refs[count + 2 : 2 * count + 2]
    rows, acc = refs[2 * count + 2 :]
    size = blocks[0].shape[1]
    step = pl.program_id(0)

    @pl.when(step == 0)
    def _():
        for at, block in enumerate(blocks):
            rows[:, at * size : (at + 1) * size, :] = block[...]
        acc[...] = jnp.zeros_like(acc)

    contract_last = (((1,), (1,)), ((), ()))
    pre = jnp.dot(rows[0], first[...], preferred_element_type=jnp.float32)
    act_grad = lax.dot_general(
        rows[1], second[...], contract_last, preferred_element_type=jnp.float32
    )
    square = pre * pre
    bent = jnp.tanh(pre * (GELU_A + GELU_B * square))
    gate = 0.5 + 0.5 * bent
    activation = (pre * gate).astype(jnp.bfloat16)
    slope = gate + (0.5 * pre) * (1.0 - bent * bent) * (GELU_A + 3.0 * GELU_B * square)
    pre_grad = (act_grad * slope).astype(jnp.bfloat16)
    acc[0] += jnp.dot(activation, second[...], preferred_element_type=jnp.float32)
    acc[1] += lax.dot_general(
        pre_grad, first[...], contract_last, preferred_element_type=jnp.float32
    )

    @pl.when(step == pl.num_programs(0) - 1)
    def _():
        for at, out in enumerate(outs):
            out[...] = acc[:, at * size : (at + 1) * size, :].astype(out.dtype)


def expert_pass(blocks, dtype, first, second):
    count = len(blocks)
    _, size, width = blocks[0].shape
    hidden = first.shape[1]
    part = 512
    whole = pl.BlockSpec((2, size, width), lambda j: (0, 0, 0))
    return pl.pallas_call(
        lambda *refs: expert_kernel(count, *refs),
        grid=(hidden // part,),
        in_specs=[whole] * count
        + [
            pl.BlockSpec((width, part), lambda j: (0, j)),
            pl.BlockSpec((part, width), lambda j: (j, 0)),
        ],
        out_specs=[whole] * count,
        out_shape=[jax.ShapeDtypeStruct((2, size, width), dtype)] * count,
        scratch_shapes=[
            pltpu.VMEM((2, count * size, width), jnp.bfloat16),
            pltpu.VMEM((2, count * size, width), jnp.float32),
        ],
        compiler_params=pltpu.CompilerParams(vmem_limit_bytes=24 * 2**20),
        cost_estimate=pl.CostEstimate(
            flops=8 * count * size * width * hidden,
            bytes_accessed=4 * width * hidden,
            transcendentals=count * size * hidden,
        ),
        name="expert_rows",
    )(*blocks, first, second)


def sum_kernel(mine_a, back_a, mine_b, back_b, out):
    out[0] = (mine_a[...] + back_a[...].astype(jnp.float32)).astype(jnp.bfloat16)
    out[1] = (mine_b[...] + back_b[...].astype(jnp.float32)).astype(jnp.bfloat16)


def sum_halves(*parts):
    return pl.pallas_call(
        sum_kernel,
        out_shape=jax.ShapeDtypeStruct((2,) + parts[0].shape, jnp.bfloat16),
        compiler_params=pltpu.CompilerParams(vmem_limit_bytes=16 * 2**20),
        cost_estimate=pl.CostEstimate(
            flops=2 * parts[0].size, bytes_accessed=16 * parts[0].size, transcendentals=0
        ),
        name="sum_halves",
    )(*parts)


def lay_out_kernel(tokens, grads, flat_tokens, turned, flat_grads):
    flat_tokens[...] = tokens[...]
    flat_grads[...] = grads[...]
    for image in range(tokens.shape[0]):
        turned[image] = tokens[image].T


def lay_out(tokens, grads):
    images, rows, width = tokens.shape
    return pl.pallas_call(
        lay_out_kernel,
        out_shape=[
            jax.ShapeDtypeStruct(tokens.shape, tokens.dtype),
            jax.ShapeDtypeStruct((images, width, rows), tokens.dtype),
            jax.ShapeDtypeStruct(grads.shape, grads.dtype),
        ],
        compiler_params=pltpu.CompilerParams(vmem_limit_bytes=16 * 2**20),
        cost_estimate=pl.CostEstimate(
            flops=0, bytes_accessed=10 * tokens.size, transcendentals=0
        ),
        name="lay_out",
    )(tokens, grads)


def grad_kernel(tokens, turned, grads, combine, dispatch, outs, backs, logit_grad, phi):
    contract_last = (((1,), (1,)), ((), ()))
    total = None
    for image in range(tokens.shape[0]):
        comb, disp = combine[image], dispatch[image]
        wide = lax.dot_general(
            grads[image], outs[image], contract_last, preferred_element_type=jnp.float32
        )
        deep = lax.dot_general(
            tokens[image], backs[image], contract_last, preferred_element_type=jnp.float32
        )
        wide = comb * (wide - jnp.sum(comb * wide, axis=1, keepdims=True))
        deep = disp * (deep - jnp.sum(disp * deep, axis=0, keepdims=True))
        grad = (wide + deep).astype(jnp.bfloat16)
        logit_grad[image] = grad
        term = jnp.dot(turned[image], grad, preferred_element_type=jnp.float32)
        total = term if total is None else total + term
    phi[...] = total.astype(jnp.bfloat16)


def logit_grads(tokens, turned, grads, combine, dispatch, outs, backs):
    images, rows, width = tokens.shape
    slots = outs.shape[1]
    return pl.pallas_call(
        grad_kernel,
        out_shape=[
            jax.ShapeDtypeStruct((images, rows, slots), jnp.bfloat16),
            jax.ShapeDtypeStruct((width, slots), jnp.bfloat16),
        ],
        compiler_params=pltpu.CompilerParams(vmem_limit_bytes=24 * 2**20),
        cost_estimate=pl.CostEstimate(
            flops=6 * images * rows * width * slots,
            bytes_accessed=8 * images * rows * width,
            transcendentals=0,
        ),
        name="logit_grads",
    )(tokens, turned, grads, combine, dispatch, outs, backs)


def local(tokens, grad_out, slot_weight, in_weight, out_weight):
    images = tokens.shape[0]
    logits = jnp.einsum("imd,dn->imn", tokens, slot_weight, preferred_element_type=jnp.float32)
    logits = lax.optimization_barrier(logits)
    dispatch = jax.nn.softmax(logits, axis=1)
    combine = jax.nn.softmax(logits, axis=2)
    dispatch_b = dispatch.astype(jnp.bfloat16)
    combine_b = combine.astype(jnp.bfloat16)
    slot_inputs = jnp.einsum(
        "imn,imd->ind", dispatch_b, tokens, preferred_element_type=jnp.float32
    ).astype(jnp.bfloat16)
    slot_grads = jnp.einsum(
        "imn,imd->ind", combine_b, grad_out, preferred_element_type=jnp.float32
    ).astype(jnp.bfloat16)
    both = jnp.stack([slot_inputs, slot_grads], axis=0)
    both = jnp.transpose(both, (2, 0, 1, 3))
    experts, _, _, width = both.shape
    both = lax.all_to_all(both, "expert", split_axis=0, concat_axis=0, tiled=True)
    both = both.reshape(2, experts // 2, 2, images, width)
    piece_a = jnp.transpose(both[0], (1, 0, 2, 3)).reshape(2, -1, width)
    piece_b = jnp.transpose(after(both, piece_a)[1], (1, 0, 2, 3)).reshape(2, -1, width)
    first, second = (
        pltpu.with_memory_space_constraint(weight[0], pltpu.HBM)
        for weight in (in_weight, out_weight)
    )
    pair_a = swap(piece_a)
    mine = expert_pass([piece_a, piece_b], jnp.float32, first, second)
    pair_b = swap(after(piece_b, mine[0]))
    early_tokens, early_grads, _ = lax.optimization_barrier((tokens, grad_out, mine[0]))
    flat_tokens, turned, flat_grads = lay_out(early_tokens, early_grads)
    (sent_a,) = expert_pass([pair_a], jnp.bfloat16, first, second)
    back_a = swap(sent_a)
    (sent_b,) = expert_pass([pair_b], jnp.bfloat16, first, second)
    back_b = swap(sent_b)
    sums = sum_halves(mine[0], back_a, mine[1], back_b)
    sums, flat_tokens, turned, flat_grads = lax.optimization_barrier(
        (sums, flat_tokens, turned, flat_grads)
    )
    sums = sums.reshape(2, 2, experts // 2, images, width)
    sums = jnp.transpose(sums, (0, 2, 1, 3, 4)).reshape(experts, 2, images, width)
    summed = lax.all_to_all(sums, "expert", split_axis=0, concat_axis=0, tiled=True)
    slot_outputs = jnp.transpose(summed[:, 0], (1, 0, 2))
    slot_in_grad = jnp.transpose(summed[:, 1], (1, 0, 2))
    logit_grad, phi_parts = logit_grads(
        flat_tokens, turned, flat_grads, combine, dispatch, slot_outputs, slot_in_grad
    )
    input_grad = jnp.einsum(
        "imn,ind->imd", dispatch_b, slot_in_grad, preferred_element_type=jnp.float32
    )
    input_grad = input_grad + jnp.einsum(
        "imn,dn->imd", logit_grad, slot_weight, preferred_element_type=jnp.float32
    )
    phi_parts = phi_parts.reshape(2 * experts, -1, experts)
    phi_parts = lax.all_to_all(phi_parts, BOTH, split_axis=0, concat_axis=0, tiled=True)
    phi_grad = jnp.sum(phi_parts.astype(jnp.float32), axis=0)
    return (input_grad.astype(jnp.bfloat16), phi_grad)


def solution(mesh):
    placed = (
        P(("expert", "hidden"), None, None),
        P(("expert", "hidden"), None, None),
        P(),
        P("expert", None, "hidden"),
        P("expert", "hidden", None),
    )
    return jax.shard_map(
        local,
        mesh=mesh,
        in_specs=placed,
        out_specs=(P(("expert", "hidden"), None, None), P(("expert", "hidden"), None)),
        check_vma=False,
    )
```

```python
import jax
import jax.numpy as jnp
from jax import lax
from jax.experimental import pallas as pl
from jax.experimental.pallas import tpu as pltpu
from jax.sharding import PartitionSpec as P

BOTH = ("expert", "hidden")
GELU_A = 0.7978845608028654
GELU_B = 0.7978845608028654 * 0.044715


def swap(block):
    return lax.ppermute(block, "hidden", [(0, 1), (1, 0)])


def after(value, *earlier):
    return lax.optimization_barrier((value,) + earlier)[0]


def expert_kernel(count, *refs):
    blocks = refs[:count]
    first, second = refs[count], refs[count + 1]
    outs = refs[count + 2 : 2 * count + 2]
    rows, acc = refs[2 * count + 2 :]
    size = blocks[0].shape[1]
    step = pl.program_id(0)

    @pl.when(step == 0)
    def _():
        for at, block in enumerate(blocks):
            rows[:, at * size : (at + 1) * size, :] = block[...]
        acc[...] = jnp.zeros_like(acc)

    contract_last = (((1,), (1,)), ((), ()))
    pre = jnp.dot(rows[0], first[...], preferred_element_type=jnp.float32)
    act_grad = lax.dot_general(
        rows[1], second[...], contract_last, preferred_element_type=jnp.float32
    )
    square = pre * pre
    bent = jnp.tanh(pre * (GELU_A + GELU_B * square))
    gate = 0.5 + 0.5 * bent
    activation = (pre * gate).astype(jnp.bfloat16)
    slope = gate + (0.5 * pre) * (1.0 - bent * bent) * (GELU_A + 3.0 * GELU_B * square)
    pre_grad = (act_grad * slope).astype(jnp.bfloat16)
    acc[0] += jnp.dot(activation, second[...], preferred_element_type=jnp.float32)
    acc[1] += lax.dot_general(
        pre_grad, first[...], contract_last, preferred_element_type=jnp.float32
    )

    @pl.when(step == pl.num_programs(0) - 1)
    def _():
        for at, out in enumerate(outs):
            out[...] = acc[:, at * size : (at + 1) * size, :].astype(out.dtype)


def expert_pass(blocks, dtype, first, second):
    count = len(blocks)
    _, size, width = blocks[0].shape
    hidden = first.shape[1]
    part = 512
    whole = pl.BlockSpec((2, size, width), lambda j: (0, 0, 0))
    return pl.pallas_call(
        lambda *refs: expert_kernel(count, *refs),
        grid=(hidden // part,),
        in_specs=[whole] * count
        + [
            pl.BlockSpec((width, part), lambda j: (0, j)),
            pl.BlockSpec((part, width), lambda j: (j, 0)),
        ],
        out_specs=[whole] * count,
        out_shape=[jax.ShapeDtypeStruct((2, size, width), dtype)] * count,
        scratch_shapes=[
            pltpu.VMEM((2, count * size, width), jnp.bfloat16),
            pltpu.VMEM((2, count * size, width), jnp.float32),
        ],
        compiler_params=pltpu.CompilerParams(vmem_limit_bytes=24 * 2**20),
        cost_estimate=pl.CostEstimate(
            flops=8 * count * size * width * hidden,
            bytes_accessed=4 * width * hidden,
            transcendentals=count * size * hidden,
        ),
        name="expert_rows",
    )(*blocks, first, second)


def sum_kernel(mine, back, out):
    out[...] = (mine[...] + back[...].astype(jnp.float32)).astype(jnp.bfloat16)


def sum_halves(mine, back):
    return pl.pallas_call(
        sum_kernel,
        out_shape=jax.ShapeDtypeStruct(back.shape, back.dtype),
        compiler_params=pltpu.CompilerParams(vmem_limit_bytes=8 * 2**20),
        cost_estimate=pl.CostEstimate(
            flops=mine.size, bytes_accessed=8 * mine.size, transcendentals=0
        ),
        name="sum_halves",
    )(mine, back)


def lay_out_kernel(tokens, grads, flat_tokens, turned, flat_grads):
    flat_tokens[...] = tokens[...]
    flat_grads[...] = grads[...]
    for image in range(tokens.shape[0]):
        turned[image] = tokens[image].T


def lay_out(tokens, grads):
    images, rows, width = tokens.shape
    return pl.pallas_call(
        lay_out_kernel,
        out_shape=[
            jax.ShapeDtypeStruct(tokens.shape, tokens.dtype),
            jax.ShapeDtypeStruct((images, width, rows), tokens.dtype),
            jax.ShapeDtypeStruct(grads.shape, grads.dtype),
        ],
        compiler_params=pltpu.CompilerParams(vmem_limit_bytes=16 * 2**20),
        cost_estimate=pl.CostEstimate(
            flops=0, bytes_accessed=10 * tokens.size, transcendentals=0
        ),
        name="lay_out",
    )(tokens, grads)


def grad_kernel(tokens, turned, grads, combine, dispatch, outs, backs, logit_grad, phi):
    contract_last = (((1,), (1,)), ((), ()))
    total = None
    for image in range(tokens.shape[0]):
        comb, disp = combine[image], dispatch[image]
        wide = lax.dot_general(
            grads[image], outs[image], contract_last, preferred_element_type=jnp.float32
        )
        deep = lax.dot_general(
            tokens[image], backs[image], contract_last, preferred_element_type=jnp.float32
        )
        wide = comb * (wide - jnp.sum(comb * wide, axis=1, keepdims=True))
        deep = disp * (deep - jnp.sum(disp * deep, axis=0, keepdims=True))
        grad = (wide + deep).astype(jnp.bfloat16)
        logit_grad[image] = grad
        term = jnp.dot(turned[image], grad, preferred_element_type=jnp.float32)
        total = term if total is None else total + term
    phi[...] = total.astype(jnp.bfloat16)


def logit_grads(tokens, turned, grads, combine, dispatch, outs, backs):
    images, rows, width = tokens.shape
    slots = outs.shape[1]
    return pl.pallas_call(
        grad_kernel,
        out_shape=[
            jax.ShapeDtypeStruct((images, rows, slots), jnp.bfloat16),
            jax.ShapeDtypeStruct((width, slots), jnp.bfloat16),
        ],
        compiler_params=pltpu.CompilerParams(vmem_limit_bytes=24 * 2**20),
        cost_estimate=pl.CostEstimate(
            flops=6 * images * rows * width * slots,
            bytes_accessed=8 * images * rows * width,
            transcendentals=0,
        ),
        name="logit_grads",
    )(tokens, turned, grads, combine, dispatch, outs, backs)


def local(tokens, grad_out, slot_weight, in_weight, out_weight):
    images = tokens.shape[0]
    logits = jnp.einsum("imd,dn->imn", tokens, slot_weight, preferred_element_type=jnp.float32)
    logits = lax.optimization_barrier(logits)
    dispatch = jax.nn.softmax(logits, axis=1)
    combine = jax.nn.softmax(logits, axis=2)
    dispatch_b = dispatch.astype(jnp.bfloat16)
    combine_b = combine.astype(jnp.bfloat16)
    slot_inputs = jnp.einsum(
        "imn,imd->ind", dispatch_b, tokens, preferred_element_type=jnp.float32
    ).astype(jnp.bfloat16)
    slot_grads = jnp.einsum(
        "imn,imd->ind", combine_b, grad_out, preferred_element_type=jnp.float32
    ).astype(jnp.bfloat16)
    both = jnp.stack([slot_inputs, slot_grads], axis=0)
    both = jnp.transpose(both, (2, 0, 1, 3))
    experts, _, _, width = both.shape
    both = lax.all_to_all(both, "expert", split_axis=0, concat_axis=0, tiled=True)
    both = both.reshape(2, experts // 2, 2, images, width)
    piece_a = jnp.transpose(both[0], (1, 0, 2, 3)).reshape(2, -1, width)
    piece_b = jnp.transpose(after(both, piece_a)[1], (1, 0, 2, 3)).reshape(2, -1, width)
    first, second = (
        pltpu.with_memory_space_constraint(weight[0], pltpu.HBM)
        for weight in (in_weight, out_weight)
    )
    pair_a = swap(piece_a)
    mine = expert_pass([piece_a, piece_b], jnp.float32, first, second)
    pair_b = swap(after(piece_b, mine[0]))
    early_tokens, early_grads, _ = lax.optimization_barrier((tokens, grad_out, mine[0]))
    flat_tokens, turned, flat_grads = lay_out(early_tokens, early_grads)
    (sent_a,) = expert_pass([pair_a], jnp.bfloat16, first, second)
    back_a = swap(sent_a)
    (sent_b,) = expert_pass([pair_b], jnp.bfloat16, first, second)
    back_b = swap(sent_b)
    def packed(mine_part, back_part):
        half = sum_halves(mine_part, back_part)
        half = half.reshape(2, experts // 2, images, width)
        return jnp.transpose(half, (1, 0, 2, 3))

    sums = jnp.pad(packed(mine[0], back_a), ((0, experts // 2), (0, 0), (0, 0), (0, 0)))
    sums, flat_tokens, turned, flat_grads, back_b = lax.optimization_barrier(
        (sums, flat_tokens, turned, flat_grads, back_b)
    )
    sums = lax.dynamic_update_slice(sums, packed(mine[1], back_b), (experts // 2, 0, 0, 0))
    summed = lax.all_to_all(sums, "expert", split_axis=0, concat_axis=0, tiled=True)
    slot_outputs = jnp.transpose(summed[:, 0], (1, 0, 2))
    slot_in_grad = jnp.transpose(summed[:, 1], (1, 0, 2))
    logit_grad, phi_parts = logit_grads(
        flat_tokens, turned, flat_grads, combine, dispatch, slot_outputs, slot_in_grad
    )
    input_grad = jnp.einsum(
        "imn,ind->imd", dispatch_b, slot_in_grad, preferred_element_type=jnp.float32
    )
    input_grad = input_grad + jnp.einsum(
        "imn,dn->imd", logit_grad, slot_weight, preferred_element_type=jnp.float32
    )
    phi_parts = phi_parts.reshape(2 * experts, -1, experts)
    phi_parts = lax.all_to_all(phi_parts, BOTH, split_axis=0, concat_axis=0, tiled=True)
    phi_grad = jnp.sum(phi_parts.astype(jnp.float32), axis=0)
    return (input_grad.astype(jnp.bfloat16), phi_grad)


def solution(mesh):
    placed = (
        P(("expert", "hidden"), None, None),
        P(("expert", "hidden"), None, None),
        P(),
        P("expert", None, "hidden"),
        P("expert", "hidden", None),
    )
    return jax.shard_map(
        local,
        mesh=mesh,
        in_specs=placed,
        out_specs=(P(("expert", "hidden"), None, None), P(("expert", "hidden"), None)),
        check_vma=False,
    )
```

```python
import jax
import jax.numpy as jnp
from jax import lax
from jax.experimental import pallas as pl
from jax.experimental.pallas import tpu as pltpu
from jax.sharding import PartitionSpec as P

BOTH = ("expert", "hidden")
GELU_A = 0.7978845608028654
GELU_B = 0.7978845608028654 * 0.044715


def swap(block):
    return lax.ppermute(block, "hidden", [(0, 1), (1, 0)])


def after(value, *earlier):
    return lax.optimization_barrier((value,) + earlier)[0]


def expert_kernel(count, *refs):
    blocks = refs[:count]
    first, second = refs[count], refs[count + 1]
    outs = refs[count + 2 : 2 * count + 2]
    rows, acc = refs[2 * count + 2 :]
    size = blocks[0].shape[1]
    step = pl.program_id(0)

    @pl.when(step == 0)
    def _():
        for at, block in enumerate(blocks):
            rows[:, at * size : (at + 1) * size, :] = block[...]
        acc[...] = jnp.zeros_like(acc)

    contract_last = (((1,), (1,)), ((), ()))
    pre = jnp.dot(rows[0], first[...], preferred_element_type=jnp.float32)
    act_grad = lax.dot_general(
        rows[1], second[...], contract_last, preferred_element_type=jnp.float32
    )
    square = pre * pre
    bent = jnp.tanh(pre * (GELU_A + GELU_B * square))
    gate = 0.5 + 0.5 * bent
    activation = (pre * gate).astype(jnp.bfloat16)
    slope = gate + (0.5 * pre) * (1.0 - bent * bent) * (GELU_A + 3.0 * GELU_B * square)
    pre_grad = (act_grad * slope).astype(jnp.bfloat16)
    acc[0] += jnp.dot(activation, second[...], preferred_element_type=jnp.float32)
    acc[1] += lax.dot_general(
        pre_grad, first[...], contract_last, preferred_element_type=jnp.float32
    )

    @pl.when(step == pl.num_programs(0) - 1)
    def _():
        for at, out in enumerate(outs):
            out[...] = acc[:, at * size : (at + 1) * size, :].astype(out.dtype)


def expert_pass(blocks, dtype, first, second):
    count = len(blocks)
    _, size, width = blocks[0].shape
    hidden = first.shape[1]
    part = 512
    whole = pl.BlockSpec((2, size, width), lambda j: (0, 0, 0))
    return pl.pallas_call(
        lambda *refs: expert_kernel(count, *refs),
        grid=(hidden // part,),
        in_specs=[whole] * count
        + [
            pl.BlockSpec((width, part), lambda j: (0, j)),
            pl.BlockSpec((part, width), lambda j: (j, 0)),
        ],
        out_specs=[whole] * count,
        out_shape=[jax.ShapeDtypeStruct((2, size, width), dtype)] * count,
        scratch_shapes=[
            pltpu.VMEM((2, count * size, width), jnp.bfloat16),
            pltpu.VMEM((2, count * size, width), jnp.float32),
        ],
        compiler_params=pltpu.CompilerParams(vmem_limit_bytes=24 * 2**20),
        cost_estimate=pl.CostEstimate(
            flops=8 * count * size * width * hidden,
            bytes_accessed=4 * width * hidden,
            transcendentals=count * size * hidden,
        ),
        name="expert_rows",
    )(*blocks, first, second)


def sum_kernel(mine, back, out):
    out[...] = (mine[...] + back[...].astype(jnp.float32)).astype(jnp.bfloat16)


def sum_halves(mine, back):
    return pl.pallas_call(
        sum_kernel,
        out_shape=jax.ShapeDtypeStruct(back.shape, back.dtype),
        compiler_params=pltpu.CompilerParams(vmem_limit_bytes=8 * 2**20),
        cost_estimate=pl.CostEstimate(
            flops=mine.size, bytes_accessed=8 * mine.size, transcendentals=0
        ),
        name="sum_halves",
    )(mine, back)


def lay_out_kernel(tokens, grads, flat_tokens, turned, flat_grads):
    flat_tokens[...] = tokens[...]
    flat_grads[...] = grads[...]
    for image in range(tokens.shape[0]):
        turned[image] = tokens[image].T


def lay_out(tokens, grads):
    images, rows, width = tokens.shape
    return pl.pallas_call(
        lay_out_kernel,
        out_shape=[
            jax.ShapeDtypeStruct(tokens.shape, tokens.dtype),
            jax.ShapeDtypeStruct((images, width, rows), tokens.dtype),
            jax.ShapeDtypeStruct(grads.shape, grads.dtype),
        ],
        compiler_params=pltpu.CompilerParams(vmem_limit_bytes=16 * 2**20),
        cost_estimate=pl.CostEstimate(
            flops=0, bytes_accessed=10 * tokens.size, transcendentals=0
        ),
        name="lay_out",
    )(tokens, grads)


def grad_kernel(tokens, turned, grads, combine, dispatch, outs, backs, logit_grad, phi):
    contract_last = (((1,), (1,)), ((), ()))
    total = None
    for image in range(tokens.shape[0]):
        comb, disp = combine[image], dispatch[image]
        wide = lax.dot_general(
            grads[image], outs[image], contract_last, preferred_element_type=jnp.float32
        )
        deep = lax.dot_general(
            tokens[image], backs[image], contract_last, preferred_element_type=jnp.float32
        )
        wide = comb * (wide - jnp.sum(comb * wide, axis=1, keepdims=True))
        deep = disp * (deep - jnp.sum(disp * deep, axis=0, keepdims=True))
        grad = (wide + deep).astype(jnp.bfloat16)
        logit_grad[image] = grad
        term = jnp.dot(turned[image], grad, preferred_element_type=jnp.float32)
        total = term if total is None else total + term
    phi[...] = total.astype(jnp.bfloat16)


def logit_grads(tokens, turned, grads, combine, dispatch, outs, backs):
    images, rows, width = tokens.shape
    slots = outs.shape[1]
    return pl.pallas_call(
        grad_kernel,
        out_shape=[
            jax.ShapeDtypeStruct((images, rows, slots), jnp.bfloat16),
            jax.ShapeDtypeStruct((width, slots), jnp.bfloat16),
        ],
        compiler_params=pltpu.CompilerParams(vmem_limit_bytes=24 * 2**20),
        cost_estimate=pl.CostEstimate(
            flops=6 * images * rows * width * slots,
            bytes_accessed=8 * images * rows * width,
            transcendentals=0,
        ),
        name="logit_grads",
    )(tokens, turned, grads, combine, dispatch, outs, backs)


def local(tokens, grad_out, slot_weight, in_weight, out_weight):
    images = tokens.shape[0]
    logits = jnp.einsum("imd,dn->imn", tokens, slot_weight, preferred_element_type=jnp.float32)
    logits = lax.optimization_barrier(logits)
    dispatch = jax.nn.softmax(logits, axis=1)
    combine = jax.nn.softmax(logits, axis=2)
    dispatch_b = dispatch.astype(jnp.bfloat16)
    combine_b = combine.astype(jnp.bfloat16)
    slot_inputs = jnp.einsum(
        "imn,imd->ind", dispatch_b, tokens, preferred_element_type=jnp.float32
    ).astype(jnp.bfloat16)
    slot_grads = jnp.einsum(
        "imn,imd->ind", combine_b, grad_out, preferred_element_type=jnp.float32
    ).astype(jnp.bfloat16)
    both = jnp.transpose(jnp.stack([slot_inputs, slot_grads], axis=0), (2, 1, 0, 3))
    experts, _, _, width = both.shape
    both = lax.all_to_all(
        both.reshape(images * experts, 2, width), BOTH, split_axis=0, concat_axis=0, tiled=True
    )
    piece_a = jnp.transpose(both[:experts], (1, 0, 2))
    piece_b = jnp.transpose(after(both, piece_a)[experts:], (1, 0, 2))
    first, second = (
        pltpu.with_memory_space_constraint(weight[0], pltpu.HBM)
        for weight in (in_weight, out_weight)
    )
    pair_a = swap(piece_a)
    mine = expert_pass([piece_a, piece_b], jnp.float32, first, second)
    pair_b = swap(after(piece_b, mine[0]))
    early_tokens, early_grads, _ = lax.optimization_barrier((tokens, grad_out, mine[0]))
    flat_tokens, turned, flat_grads = lay_out(early_tokens, early_grads)
    (sent_a,) = expert_pass([pair_a], jnp.bfloat16, first, second)
    back_a = swap(sent_a)
    (sent_b,) = expert_pass([pair_b], jnp.bfloat16, first, second)
    back_b = swap(sent_b)
    def packed(mine_part, back_part):
        return jnp.transpose(sum_halves(mine_part, back_part), (1, 0, 2))

    sums = jnp.pad(packed(mine[0], back_a), ((0, experts), (0, 0), (0, 0)))
    sums, flat_tokens, turned, flat_grads, back_b = lax.optimization_barrier(
        (sums, flat_tokens, turned, flat_grads, back_b)
    )
    sums = lax.dynamic_update_slice(sums, packed(mine[1], back_b), (experts, 0, 0))
    summed = lax.all_to_all(sums, BOTH, split_axis=0, concat_axis=0, tiled=True)
    summed = jnp.transpose(summed.reshape(experts, images, 2, width), (2, 1, 0, 3))
    slot_outputs, slot_in_grad = summed[0], summed[1]
    logit_grad, phi_parts = logit_grads(
        flat_tokens, turned, flat_grads, combine, dispatch, slot_outputs, slot_in_grad
    )
    input_grad = jnp.einsum(
        "imn,ind->imd", dispatch_b, slot_in_grad, preferred_element_type=jnp.float32
    )
    input_grad = input_grad + jnp.einsum(
        "imn,dn->imd", logit_grad, slot_weight, preferred_element_type=jnp.float32
    )
    phi_parts = phi_parts.reshape(2 * experts, -1, experts)
    phi_parts = lax.all_to_all(phi_parts, BOTH, split_axis=0, concat_axis=0, tiled=True)
    phi_grad = jnp.sum(phi_parts.astype(jnp.float32), axis=0)
    return (input_grad.astype(jnp.bfloat16), phi_grad)


def solution(mesh):
    placed = (
        P(("expert", "hidden"), None, None),
        P(("expert", "hidden"), None, None),
        P(),
        P("expert", None, "hidden"),
        P("expert", "hidden", None),
    )
    return jax.shard_map(
        local,
        mesh=mesh,
        in_specs=placed,
        out_specs=(P(("expert", "hidden"), None, None), P(("expert", "hidden"), None)),
        check_vma=False,
    )
```

```python
import jax
import jax.numpy as jnp
from jax import lax
from jax.experimental import pallas as pl
from jax.experimental.pallas import tpu as pltpu
from jax.sharding import PartitionSpec as P

BOTH = ("expert", "hidden")
GELU_A = 0.7978845608028654
GELU_B = 0.7978845608028654 * 0.044715


def swap(block):
    return lax.ppermute(block, "hidden", [(0, 1), (1, 0)])


def after(value, *earlier):
    return lax.optimization_barrier((value,) + earlier)[0]


def expert_kernel(count, *refs):
    blocks = refs[:count]
    first, second = refs[count], refs[count + 1]
    outs = refs[count + 2 : 2 * count + 2]
    rows, acc = refs[2 * count + 2 :]
    size = blocks[0].shape[1]
    step = pl.program_id(0)

    @pl.when(step == 0)
    def _():
        for at, block in enumerate(blocks):
            rows[:, at * size : (at + 1) * size, :] = block[...]
        acc[...] = jnp.zeros_like(acc)

    contract_last = (((1,), (1,)), ((), ()))
    pre = jnp.dot(rows[0], first[...], preferred_element_type=jnp.float32)
    act_grad = lax.dot_general(
        rows[1], second[...], contract_last, preferred_element_type=jnp.float32
    )
    square = pre * pre
    bent = jnp.tanh(pre * (GELU_A + GELU_B * square))
    gate = 0.5 + 0.5 * bent
    activation = (pre * gate).astype(jnp.bfloat16)
    slope = gate + (0.5 * pre) * (1.0 - bent * bent) * (GELU_A + 3.0 * GELU_B * square)
    pre_grad = (act_grad * slope).astype(jnp.bfloat16)
    acc[0] += jnp.dot(activation, second[...], preferred_element_type=jnp.float32)
    acc[1] += lax.dot_general(
        pre_grad, first[...], contract_last, preferred_element_type=jnp.float32
    )

    @pl.when(step == pl.num_programs(0) - 1)
    def _():
        for at, out in enumerate(outs):
            out[...] = acc[:, at * size : (at + 1) * size, :].astype(out.dtype)


def expert_pass(blocks, dtype, first, second):
    count = len(blocks)
    _, size, width = blocks[0].shape
    hidden = first.shape[1]
    part = 512
    whole = pl.BlockSpec((2, size, width), lambda j: (0, 0, 0))
    return pl.pallas_call(
        lambda *refs: expert_kernel(count, *refs),
        grid=(hidden // part,),
        in_specs=[whole] * count
        + [
            pl.BlockSpec((width, part), lambda j: (0, j)),
            pl.BlockSpec((part, width), lambda j: (j, 0)),
        ],
        out_specs=[whole] * count,
        out_shape=[jax.ShapeDtypeStruct((2, size, width), dtype)] * count,
        scratch_shapes=[
            pltpu.VMEM((2, count * size, width), jnp.bfloat16),
            pltpu.VMEM((2, count * size, width), jnp.float32),
        ],
        compiler_params=pltpu.CompilerParams(vmem_limit_bytes=24 * 2**20),
        cost_estimate=pl.CostEstimate(
            flops=8 * count * size * width * hidden,
            bytes_accessed=4 * width * hidden,
            transcendentals=count * size * hidden,
        ),
        name="expert_rows",
    )(*blocks, first, second)


def sum_kernel(mine, back, out):
    out[...] = (mine[...] + back[...].astype(jnp.float32)).astype(jnp.bfloat16)


def sum_halves(mine, back):
    return pl.pallas_call(
        sum_kernel,
        out_shape=jax.ShapeDtypeStruct(back.shape, back.dtype),
        compiler_params=pltpu.CompilerParams(vmem_limit_bytes=8 * 2**20),
        cost_estimate=pl.CostEstimate(
            flops=mine.size, bytes_accessed=8 * mine.size, transcendentals=0
        ),
        name="sum_halves",
    )(mine, back)


def lay_out_kernel(
    tokens, grads, combine, dispatch, flat_tokens, turned, flat_grads, near_combine, near_dispatch
):
    near_combine[...] = combine[...]
    near_dispatch[...] = dispatch[...]
    flat_tokens[...] = tokens[...]
    flat_grads[...] = grads[...]
    for image in range(tokens.shape[0]):
        turned[image] = tokens[image].T


def lay_out(tokens, grads, combine, dispatch):
    images, rows, width = tokens.shape
    return pl.pallas_call(
        lay_out_kernel,
        out_shape=[
            jax.ShapeDtypeStruct(tokens.shape, tokens.dtype),
            jax.ShapeDtypeStruct((images, width, rows), tokens.dtype),
            jax.ShapeDtypeStruct(grads.shape, grads.dtype),
            jax.ShapeDtypeStruct(combine.shape, combine.dtype),
            jax.ShapeDtypeStruct(dispatch.shape, dispatch.dtype),
        ],
        compiler_params=pltpu.CompilerParams(vmem_limit_bytes=16 * 2**20),
        cost_estimate=pl.CostEstimate(
            flops=0, bytes_accessed=10 * tokens.size, transcendentals=0
        ),
        name="lay_out",
    )(tokens, grads, combine, dispatch)


def grad_kernel(tokens, turned, grads, combine, dispatch, outs, backs, logit_grad, phi):
    contract_last = (((1,), (1,)), ((), ()))
    total = None
    for image in range(tokens.shape[0]):
        comb, disp = combine[image], dispatch[image]
        wide = lax.dot_general(
            grads[image], outs[image], contract_last, preferred_element_type=jnp.float32
        )
        deep = lax.dot_general(
            tokens[image], backs[image], contract_last, preferred_element_type=jnp.float32
        )
        wide = comb * (wide - jnp.sum(comb * wide, axis=1, keepdims=True))
        deep = disp * (deep - jnp.sum(disp * deep, axis=0, keepdims=True))
        grad = (wide + deep).astype(jnp.bfloat16)
        logit_grad[image] = grad
        term = jnp.dot(turned[image], grad, preferred_element_type=jnp.float32)
        total = term if total is None else total + term
    phi[...] = total.astype(jnp.bfloat16)


def logit_grads(tokens, turned, grads, combine, dispatch, outs, backs):
    images, rows, width = tokens.shape
    slots = outs.shape[1]
    return pl.pallas_call(
        grad_kernel,
        out_shape=[
            jax.ShapeDtypeStruct((images, rows, slots), jnp.bfloat16),
            jax.ShapeDtypeStruct((width, slots), jnp.bfloat16),
        ],
        compiler_params=pltpu.CompilerParams(vmem_limit_bytes=24 * 2**20),
        cost_estimate=pl.CostEstimate(
            flops=6 * images * rows * width * slots,
            bytes_accessed=8 * images * rows * width,
            transcendentals=0,
        ),
        name="logit_grads",
    )(tokens, turned, grads, combine, dispatch, outs, backs)


def slot_kernel(tokens, grads, weight, dispatch_b, dispatch, combine, slots):
    for image in range(tokens.shape[0]):
        own = tokens[image]
        logits = jnp.dot(own, weight[...], preferred_element_type=jnp.float32)
        disp = jnp.exp(logits - jnp.max(logits, axis=0, keepdims=True))
        disp = disp / jnp.sum(disp, axis=0, keepdims=True)
        comb = jnp.exp(logits - jnp.max(logits, axis=1, keepdims=True))
        comb = comb / jnp.sum(comb, axis=1, keepdims=True)
        dispatch[image] = disp
        combine[image] = comb
        dispatch_b[image] = disp.astype(jnp.bfloat16)
        slots[0, image] = jnp.dot(
            disp.T.astype(jnp.bfloat16), own, preferred_element_type=jnp.float32
        ).astype(jnp.bfloat16)
        slots[1, image] = jnp.dot(
            comb.T.astype(jnp.bfloat16), grads[image], preferred_element_type=jnp.float32
        ).astype(jnp.bfloat16)


def slot_rows(tokens, grads, weight):
    images, rows, width = tokens.shape
    count = weight.shape[1]
    wide = jax.ShapeDtypeStruct((images, rows, count), jnp.float32)
    return pl.pallas_call(
        slot_kernel,
        out_shape=[
            jax.ShapeDtypeStruct((images, rows, count), jnp.bfloat16),
            wide,
            wide,
            jax.ShapeDtypeStruct((2, images, count, width), jnp.bfloat16),
        ],
        compiler_params=pltpu.CompilerParams(vmem_limit_bytes=16 * 2**20),
        cost_estimate=pl.CostEstimate(
            flops=6 * images * rows * width * count,
            bytes_accessed=8 * images * rows * width,
            transcendentals=2 * images * rows * count,
        ),
        name="slot_rows",
    )(tokens, grads, weight)


def local(tokens, grad_out, slot_weight, in_weight, out_weight):
    images = tokens.shape[0]
    dispatch_b, dispatch, combine, slots = slot_rows(tokens, grad_out, slot_weight)
    both = jnp.transpose(slots, (2, 1, 0, 3))
    experts, _, _, width = both.shape
    both = lax.all_to_all(
        both.reshape(images * experts, 2, width), BOTH, split_axis=0, concat_axis=0, tiled=True
    )
    piece_a = jnp.transpose(both[:experts], (1, 0, 2))
    piece_b = jnp.transpose(after(both, piece_a)[experts:], (1, 0, 2))
    first, second = (
        pltpu.with_memory_space_constraint(weight[0], pltpu.HBM)
        for weight in (in_weight, out_weight)
    )
    pair_a = swap(piece_a)
    mine = expert_pass([piece_a, piece_b], jnp.float32, first, second)
    pair_b = swap(after(piece_b, mine[0]))
    early = lax.optimization_barrier((tokens, grad_out, combine, dispatch, mine[0]))
    placed = lay_out(*early[:4])
    (sent_a,) = expert_pass([pair_a], jnp.bfloat16, first, second)
    back_a = swap(sent_a)
    (sent_b,) = expert_pass([pair_b], jnp.bfloat16, first, second)
    back_b = swap(sent_b)
    def packed(mine_part, back_part):
        return jnp.transpose(sum_halves(mine_part, back_part), (1, 0, 2))

    sums = jnp.pad(packed(mine[0], back_a), ((0, experts), (0, 0), (0, 0)))
    sums, back_b, *placed = lax.optimization_barrier((sums, back_b, *placed))
    sums = lax.dynamic_update_slice(sums, packed(mine[1], back_b), (experts, 0, 0))
    summed = lax.all_to_all(sums, BOTH, split_axis=0, concat_axis=0, tiled=True)
    summed = jnp.transpose(summed.reshape(experts, images, 2, width), (2, 1, 0, 3))
    slot_outputs, slot_in_grad = summed[0], summed[1]
    logit_grad, phi_parts = logit_grads(*placed, slot_outputs, slot_in_grad)
    input_grad = jnp.einsum(
        "imn,ind->imd", dispatch_b, slot_in_grad, preferred_element_type=jnp.float32
    )
    input_grad = input_grad + jnp.einsum(
        "imn,dn->imd", logit_grad, slot_weight, preferred_element_type=jnp.float32
    )
    phi_parts = phi_parts.reshape(2 * experts, -1, experts)
    phi_parts = lax.all_to_all(phi_parts, BOTH, split_axis=0, concat_axis=0, tiled=True)
    phi_grad = jnp.sum(phi_parts.astype(jnp.float32), axis=0)
    return (input_grad.astype(jnp.bfloat16), phi_grad)


def solution(mesh):
    placed = (
        P(("expert", "hidden"), None, None),
        P(("expert", "hidden"), None, None),
        P(),
        P("expert", None, "hidden"),
        P("expert", "hidden", None),
    )
    return jax.shard_map(
        local,
        mesh=mesh,
        in_specs=placed,
        out_specs=(P(("expert", "hidden"), None, None), P(("expert", "hidden"), None)),
        check_vma=False,
    )
```
